256 devices in a mesh: blk: 16 (over z, x_hi), slab: 16 (over x_lo, y, core).
Axes of the slice: x: 4 (x_hi: 2, x_lo: 2; x = x_hi * 2 + x_lo), y: 4, z: 8, core: 2. Of those that a mesh axis runs over, the one named last changes fastest.
Arguments:
- orbitals: float32 [64, 48, 48, 240], P('blk', 'slab'), may hold values from -7 to 7
- kernel: float32 [48, 48, 240], replicated, may hold values from 0.02 to 25, as said below
Outputs:
- exchange_terms: float32 [64, 48, 48, 240], P('blk', 'slab')
- margin: float32 [64, 64], P(None, 'blk')
The draws below stay inside these ranges and needn't reach their ends.
Inputs may be any that keep to these rules, and one draw needn't show every extreme that they name: kernel is positive and even in each frequency index: kernel[a, b, c] equals kernel[(48 - a) mod 48, b, c], kernel[a, (48 - b) mod 48, c] and kernel[a, b, (240 - c) mod 240].
All inputs are finite; a program needn't handle non-finite values.
Results may differ from the reference program's by a relative error of at most 0.0003.
Values sent between devices are 32-bit elements; how exact they have to be, the bound alone decides.
No kernel may reach another device: no remote copies, remote signals or barrier semaphores. Data moves between devices by JAX's collectives and lax.ppermute only.
A program may use at most 128 MiB of HBM per device.

```python
import jax
import jax.numpy as jnp
from jax import lax

NX = 48
NY = 48
NZ = 240
BAND_DEV = 4
BANDS = 64


def folded(length):
    position = jnp.arange(length, dtype=jnp.int32)
    return jnp.minimum(position, length - position)


def draw_orbitals(key, part):
    key = jax.random.fold_in(key, 11)
    noise_key, common_key, weight_key = jax.random.split(key, 3)
    position = jnp.arange(NX, dtype=jnp.float32)[None, :, None, None] / NX
    noise_part = 0.8 * jax.random.truncated_normal(noise_key, -4.0, 4.0, (BANDS, NX, NY, NZ), jnp.float32)
    common = jax.random.truncated_normal(common_key, -4.0, 4.0, (1, NX, NY, NZ), jnp.float32)
    profile = 0.5 + position
    weights = jax.random.uniform(weight_key, (BANDS, 1, 1, 1), jnp.float32, -0.6, 0.6)
    return noise_part + weights * profile * common


def draw_kernel(key, part):
    key = jax.random.fold_in(key, 23)
    table_shape = (NX // 2 + 1, NY // 2 + 1, NZ // 2 + 1)
    factors = jnp.exp(jax.random.uniform(key, table_shape, jnp.float32, -0.693, 0.693))
    strength = 4.0
    offset = 1.0
    index_x = folded(NX)
    index_y = folded(NY)
    index_z = folded(NZ)
    spread = jnp.take(jnp.take(jnp.take(factors, index_x, axis=0), index_y, axis=1), index_z, axis=2)
    along_x = index_x.astype(jnp.float32)[:, None, None]
    along_y = index_y.astype(jnp.float32)[None, :, None]
    along_z = index_z.astype(jnp.float32)[None, None, :] / 5.0
    squared = along_x * along_x + along_y * along_y + along_z * along_z
    return strength * spread / jnp.sqrt(offset + squared)


def setup_inputs(seed: int = 0) -> dict:
    keys = jax.random.split(jax.random.key(seed), 3)
    return {
        "orbitals": draw_orbitals(jax.random.fold_in(keys[2], 71), 0),
        "kernel": draw_kernel(jax.random.fold_in(keys[2], 71), 0),
    }


def reference(orbitals, kernel):
    block_count = BANDS // BAND_DEV
    blocks = orbitals.reshape(block_count, BAND_DEV, NX, NY, NZ)

    def one_block(block_index):
        targets = blocks[block_index]
        before = blocks[(block_index - 1) % block_count]
        farther = blocks[(block_index - 2) % block_count]
        sources = jnp.concatenate([targets, before, farther], axis=0)
        spectra = jnp.fft.fftn(targets[:, None] * sources[None], axes=(2, 3, 4))
        potential = jnp.real(jnp.fft.ifftn(spectra * kernel, axes=(2, 3, 4)))
        return -jnp.sum(potential * sources[None], axis=1)

    block_terms = lax.map(one_block, jnp.arange(block_count, dtype=jnp.int32))
    exchange_terms = block_terms.reshape(BANDS, NX, NY, NZ)
    flat_orbitals = orbitals.reshape(BANDS, NX * NY * NZ)
    flat_terms = exchange_terms.reshape(BANDS, NX * NY * NZ)
    margin = jnp.dot(flat_orbitals, flat_terms.T, precision=lax.Precision.HIGHEST, preferred_element_type=jnp.float32) / (NX * NY * NZ)
    return exchange_terms, margin
```

```python
import functools
import math

import jax
import jax.numpy as jnp
import ml_dtypes
import numpy as np
from jax import lax
from jax.experimental import pallas as pl
from jax.experimental.pallas import tpu as pltpu
from jax.sharding import Mesh, PartitionSpec as P

NX = 48
NY = 48
NZ = 240
LANES = 256
EVEN = 26
ODD = 24
GRID = NX * NY * NZ

bf16 = jnp.bfloat16
f32 = jnp.float32
highest = lax.Precision.HIGHEST


def halves(table):
    high = table.astype(ml_dtypes.bfloat16)
    low = (table - high.astype(np.float64)).astype(ml_dtypes.bfloat16)
    return high, low


def cas(length):
    position = np.arange(length)
    angles = (position[:, None] * position[None, :] % length) * (2.0 * math.pi / length)
    return np.cos(angles) + np.sin(angles)


def left_table(table):
    high, low = halves(table)
    return np.concatenate([high, low, high], axis=1)


def make_tables():
    table_z = np.zeros((LANES, LANES))
    table_z[:NZ, :NZ] = cas(NZ)
    high, low = halves(table_z)
    along_z = np.concatenate([high, high, low], axis=0)
    along_y = left_table(np.kron(np.eye(4), cas(NY)))
    place = np.arange(NX // 2 + 1)
    angles = (place[:, None] * place[None, :] % NX) * (2.0 * math.pi / NX)
    even = np.zeros((EVEN, EVEN))
    even[:25, :25] = np.cos(angles)
    odd = np.zeros((ODD, ODD))
    odd[:24, :24] = np.sin(angles)[:24, :24]
    weight = np.full(EVEN, 2.0)
    weight[0] = weight[24] = 1.0
    eye = np.eye(8)
    even_there = left_table(np.kron(even, eye))
    odd_there = left_table(np.kron(odd, eye))
    even_back = left_table(np.kron(even * weight[None, :] * (-1.0 / GRID), eye))
    odd_back = left_table(np.kron(odd * (-2.0 / GRID), eye))
    return along_z, along_y, even_there, odd_there, even_back, odd_back


def split(value):
    high = value.astype(bf16)
    low = (value - high.astype(f32)).astype(bf16)
    return high, low


def from_right(rows, table):
    high, low = split(rows)
    return jnp.dot(jnp.concatenate([high, low, high], axis=1), table, preferred_element_type=f32)


def from_left(table, rows):
    high, low = split(rows)
    return jnp.dot(table, jnp.concatenate([high, high, low], axis=0), preferred_element_type=f32)


def widen(value):
    return jnp.pad(value, [(0, 0)] * (value.ndim - 1) + [(0, LANES - NZ)])


def pair_kernel(first, last, *refs):
    refs = list(refs)
    place = refs.pop(0)
    target_parts = [refs.pop(0) for _ in range(4)]
    source_parts = [refs.pop(0) for _ in range(4)]
    kernel_hbm = refs.pop(0)
    tables = [refs.pop(0) for _ in range(6)]
    carried = None if first else refs.pop(0)
    outs = [refs.pop(0) for _ in range(4 if last else 1)]
    target, source, filt, total, planes, sems = refs
    along_z, along_y, even_there, odd_there, even_back, odd_back = tables
    xl, y, core = place[0], place[1], place[2]

    def base(i, r, j):
        return (xl ^ i) * 24 + ((y + r) % 4) * 6 + (core ^ j) * 3

    copies = []
    for r in range(4):
        for i in range(2):
            for j in range(2):
                copies.append(
                    pltpu.make_async_copy(
                        target_parts[r].at[i, j], target.at[pl.ds(base(i, 4 - r, j), 3)], sems.at[0]
                    )
                )
                copies.append(
                    pltpu.make_async_copy(
                        source_parts[2 * i + j].at[r], source.at[pl.ds(base(i, 4 - r, j), 3)], sems.at[0]
                    )
                )
    filt_copy = pltpu.make_async_copy(kernel_hbm.at[pl.ds(0, EVEN)], filt, sems.at[1])
    for copy in copies:
        copy.start()
    filt_copy.start()
    if not first:
        carry_copy = pltpu.make_async_copy(carried, total, sems.at[2])
        carry_copy.start()
    planes[25] = jnp.zeros((NY, LANES), f32)
    planes[EVEN] = jnp.zeros((NY, LANES), f32)
    for copy in copies:
        copy.wait()

    def pair(x):
        return target[x] * source[x]

    def members(k):
        if k < 11:
            a = 2 * k + 1
            return (a, a + 1, EVEN + a, EVEN + a + 1)
        return (0, 24, 23, EVEN + 23)

    for k in range(12):
        if k < 11:
            a = 2 * k + 1
            fa, ga, fb, gb = pair(a), pair(NX - a), pair(a + 1), pair(NX - a - 1)
            rows = [fa + ga, fb + gb, fa - ga, fb - gb]
        else:
            fa, ga = pair(23), pair(25)
            rows = [pair(0), pair(24), fa + ga, fa - ga]
        rows = widen(jnp.concatenate(rows, axis=0))
        rows = from_right(rows, along_z[...])
        rows = from_left(along_y[...], rows).reshape(4, NY, LANES)
        for m, plane in enumerate(members(k)):
            planes[plane] = rows[m]

    filt_copy.wait()
    for t in range(6):
        band = pl.ds(8 * t, 8)
        screen = widen(filt[:, band, :])
        for there, back, lo, count in ((even_there, even_back, 0, EVEN), (odd_there, odd_back, EVEN, ODD)):
            rows = planes[lo : lo + count, band, :].reshape(count * 8, LANES)
            rows = from_left(there[...], rows)
            rows = rows * screen[:count].reshape(count * 8, LANES)
            rows = from_left(back[...], rows)
            planes[lo : lo + count, band, :] = rows.reshape(count, 8, LANES)

    if not first:
        carry_copy.wait()

    def add(x, value):
        value = value[:, :NZ] * source[x]
        total[x] = value if first else total[x] + value

    for k in range(12):
        rows = jnp.concatenate([planes[plane] for plane in members(k)], axis=0)
        rows = from_left(along_y[...], rows)
        rows = from_right(rows, along_z[...]).reshape(4, NY, LANES)
        if k < 11:
            a = 2 * k + 1
            for m in range(2):
                add(a + m, rows[m] + rows[m + 2])
                add(NX - a - m, rows[m] - rows[m + 2])
        else:
            add(0, rows[0])
            add(24, rows[1])
            add(23, rows[2] + rows[3])
            add(25, rows[2] - rows[3])

    copies = []
    if last:
        for r in range(4):
            for i in range(2):
                for j in range(2):
                    copies.append(
                        pltpu.make_async_copy(
                            total.at[pl.ds(base(i, r, j), 3)], outs[r].at[i, j], sems.at[3]
                        )
                    )
    else:
        copies.append(pltpu.make_async_copy(total, outs[0], sems.at[3]))
    for copy in copies:
        copy.start()
    for copy in copies:
        copy.wait()


def pair_terms(place, target_parts, source_parts, kernel, tables, carried, last):
    first = carried is None
    any_space = pl.BlockSpec(memory_space=pl.ANY)
    vmem = pl.BlockSpec(memory_space=pltpu.VMEM)
    smem = pl.BlockSpec(memory_space=pltpu.SMEM)
    operands = [place, *target_parts, *source_parts, kernel, *tables]
    specs = [smem] + [any_space] * 9 + [vmem] * 6
    if not first:
        operands.append(carried)
        specs.append(any_space)
    if last:
        out_shape = [jax.ShapeDtypeStruct((2, 2, 3, NY, NZ), f32)] * 4
        out_specs = [any_space] * 4
    else:
        out_shape = jax.ShapeDtypeStruct((NX, NY, NZ), f32)
        out_specs = any_space
    return pl.pallas_call(
        functools.partial(pair_kernel, first, last),
        out_shape=out_shape,
        in_specs=specs,
        out_specs=out_specs,
        scratch_shapes=[
            pltpu.VMEM((NX, NY, NZ), f32),
            pltpu.VMEM((NX, NY, NZ), f32),
            pltpu.VMEM((EVEN, NY, NZ), f32),
            pltpu.VMEM((NX, NY, NZ), f32),
            pltpu.VMEM((EVEN + ODD, NY, LANES), f32),
            pltpu.SemaphoreType.DMA((4,)),
        ],
        compiler_params=pltpu.CompilerParams(vmem_limit_bytes=40 * 2**20),
        cost_estimate=pl.CostEstimate(
            flops=2 * 18 * 2304 * 256 * 256, bytes_accessed=5 * GRID * 4, transcendentals=0
        ),
        name="pair_terms",
    )(*operands)


def moved(array, axes, step):
    size = lax.axis_size(axes)
    return lax.ppermute(array, axes, [(i, (i + step) % size) for i in range(size)])


def pick(array, index):
    return lax.dynamic_index_in_dim(array, index, 0, keepdims=False)


def local(orbitals, kernel):
    xh, xl, y, core = [lax.axis_index(name) for name in ("xh", "xl", "y", "core")]
    place = jnp.stack([xl, y, core]).astype(jnp.int32)
    tables = [jnp.asarray(table) for table in make_tables()]

    with jax.named_scope("source_slabs"):
        pieces = [pick(orbitals, y)]
        for r in range(1, 4):
            pieces.append(moved(pick(orbitals, (y + r) % 4), "y", r))
        own = jnp.stack(pieces)

    with jax.named_scope("target_slabs"):
        def band(i, j):
            return pick(orbitals, 2 * (xl ^ i) + (core ^ j))

        kept = [band(0, 0), band(1, 0)]
        came = moved(jnp.stack([band(0, 1), band(1, 1)]), "core", 1)
        across = moved(jnp.stack([kept[1], came[1]]), "xl", 1)
        part = jnp.stack([jnp.stack([kept[0], came[0]]), across])
        target_parts = [part] + [moved(part, "y", r) for r in range(1, 4)]

    with jax.named_scope("source_fields"):
        near = moved(own, ("z", "xh"), 1)
        far = moved(own, "z", 1)
        fields = []
        for slabs in (own, near, far):
            other = moved(slabs, "xl", 1)
            fields.append([slabs, moved(slabs, "core", 1), other, moved(other, "core", 1)])

    with jax.named_scope("all_orbitals"):
        def half(array, h):
            return lax.dynamic_slice_in_dim(array, h * (NY // 2), NY // 2, 2)

        mine = half(orbitals, xh)
        theirs = moved(half(orbitals, 1 - xh), "xh", 1)
        both = jnp.where(xh == 0, jnp.stack([mine, theirs]), jnp.stack([theirs, mine]))
        everything = lax.all_gather(both, "z", axis=0, tiled=False)

    total = pair_terms(place, target_parts, fields[0], kernel, tables, None, False)
    total = pair_terms(place, target_parts, fields[1], kernel, tables, total, False)
    partial = pair_terms(place, target_parts, fields[2], kernel, tables, total, True)

    with jax.named_scope("sum_partials"):
        summed = partial[0]
        for r in range(1, 4):
            summed = summed + moved(partial[r], "y", r)

    with jax.named_scope("to_slabs"):
        came = moved(summed[:, 1], "core", 1)
        across = moved(jnp.stack([summed[1, 0], came[1]]), "xl", 1)
        relative = jnp.stack([summed[0, 0], came[0], across[0], across[1]])
        here = 2 * xl + core
        exchange_terms = jnp.stack([pick(relative, b ^ here) for b in range(4)])

    with jax.named_scope("margin"):
        mine = half(exchange_terms, xh)
        theirs = moved(half(exchange_terms, 1 - xh), "xh", 1)
        terms = jnp.stack([mine, theirs])
        products = jnp.einsum("zhbxyw,gkxyw->gzhbk", everything, terms, precision=highest)
        products = products.reshape(2, 256)
        ordered = jnp.where(xh == 0, products, products[::-1])
        sent = jnp.broadcast_to(ordered[:, None], (2, 16, 256)).reshape(32, 256)
        got = lax.all_to_all(sent, ("xh", "xl", "y", "core"), split_axis=0, concat_axis=0, tiled=True)
        margin = jnp.sum(got, axis=0).reshape(64, 4) * (1.0 / GRID)
    return exchange_terms, margin


def solution(mesh):
    fine = Mesh(mesh.devices.reshape(8, 2, 2, 4, 2), ("z", "xh", "xl", "y", "core"))
    blk = ("z", "xh")
    slab = ("xl", "y", "core")
    return jax.shard_map(
        local,
        mesh=fine,
        in_specs=(P(blk, slab, None, None), P()),
        out_specs=(P(blk, slab, None, None), P(None, blk)),
        check_vma=False,
    )
```

```python
import functools
import math

import jax
import jax.numpy as jnp
import ml_dtypes
import numpy as np
from jax import lax
from jax.experimental import pallas as pl
from jax.experimental.pallas import tpu as pltpu
from jax.sharding import Mesh, PartitionSpec as P

NX = 48
NY = 48
NZ = 240
LANES = 256
EVEN = 26
ODD = 24
GRID = NX * NY * NZ

bf16 = jnp.bfloat16
f32 = jnp.float32
highest = lax.Precision.HIGHEST


def halves(table):
    high = table.astype(ml_dtypes.bfloat16)
    low = (table - high.astype(np.float64)).astype(ml_dtypes.bfloat16)
    return high, low


def cas(length):
    position = np.arange(length)
    angles = (position[:, None] * position[None, :] % length) * (2.0 * math.pi / length)
    return np.cos(angles) + np.sin(angles)


def left_table(table):
    high, low = halves(table)
    return np.concatenate([high, low, high], axis=1)


WIDTH = 3 * LANES
ROWS = (LANES, 192, 8 * EVEN, 8 * ODD, 8 * EVEN, 8 * ODD)
FIRST = tuple(sum(ROWS[:k]) for k in range(len(ROWS) + 1))


def make_table():
    table_z = np.zeros((LANES, LANES))
    table_z[:NZ, :NZ] = cas(NZ)
    high, low = halves(table_z)
    along_z = np.concatenate([high, high, low], axis=1)
    along_y = left_table(np.kron(np.eye(4), cas(NY)))
    place = np.arange(NX // 2 + 1)
    angles = (place[:, None] * place[None, :] % NX) * (2.0 * math.pi / NX)
    even = np.zeros((EVEN, EVEN))
    even[:25, :25] = np.cos(angles)
    odd = np.zeros((ODD, ODD))
    odd[:24, :24] = np.sin(angles)[:24, :24]
    weight = np.full(EVEN, 2.0)
    weight[0] = weight[24] = 1.0
    eye = np.eye(8)
    even_there = left_table(np.kron(even, eye))
    odd_there = left_table(np.kron(odd, eye))
    even_back = left_table(np.kron(even * weight[None, :] * (-1.0 / GRID), eye))
    odd_back = left_table(np.kron(odd * (-2.0 / GRID), eye))
    table = np.zeros((FIRST[-1], WIDTH), ml_dtypes.bfloat16)
    parts = (along_z, along_y, even_there, odd_there, even_back, odd_back)
    for first, part in zip(FIRST, parts):
        table[first : first + part.shape[0], : part.shape[1]] = part
    return table


def split(value):
    high = value.astype(bf16)
    low = (value - high.astype(f32)).astype(bf16)
    return high, low


def from_right(rows, table):
    high, low = split(rows)
    result = jnp.dot(high, table[0:LANES, 0:LANES], preferred_element_type=f32)
    result += jnp.dot(low, table[0:LANES, LANES : 2 * LANES], preferred_element_type=f32)
    return result + jnp.dot(high, table[0:LANES, 2 * LANES :], preferred_element_type=f32)


def from_left(table, k, rows):
    high, low = split(rows)
    stacked = jnp.concatenate([high, high, low], axis=0)
    return jnp.dot(
        table[FIRST[k] : FIRST[k + 1], : stacked.shape[0]], stacked, preferred_element_type=f32
    )


def widen(value):
    return jnp.pad(value, [(0, 0)] * (value.ndim - 1) + [(0, LANES - NZ)])


def pair_kernel(count, last, *refs):
    refs = list(refs)
    place, table_hbm, filt_hbm = refs[:3]
    target_parts, refs = refs[3:8], refs[8:]
    field_parts, refs = [refs[4 * s : 4 * s + 4] for s in range(count)], refs[4 * count :]
    if last:
        carried, up_first, down_first, up_second, down_second, keep = refs[:6]
        refs = refs[6:]
    else:
        out, refs = refs[0], refs[1:]
    targets, sources, source, product, planes, total, table, filt, sems = refs
    xl, y, core = place[0], place[1], place[2]

    part, lower, low_far, high_far, upper = target_parts
    table_copy = pltpu.make_async_copy(table_hbm, table, sems.at[3])
    filt_copy = pltpu.make_async_copy(filt_hbm.at[pl.ds(0, EVEN)], filt, sems.at[4])
    target_copies = [
        pltpu.make_async_copy(ref, dst, sems.at[5])
        for ref, dst in (
            (part, targets.at[0]),
            (lower, targets.at[1]),
            (low_far, targets.at[2, 0]),
            (high_far, targets.at[2, 1]),
            (upper, targets.at[3]),
        )
    ]
    source_copies = [
        pltpu.make_async_copy(ref, sources.at[s, q], sems.at[s])
        for s, parts in enumerate(field_parts)
        for q, ref in enumerate(parts)
    ]
    carry_copies = [pltpu.make_async_copy(carried, total, sems.at[2])] if last else []
    for copy in target_copies + source_copies[:4] + [table_copy, filt_copy] + source_copies[4:] + carry_copies:
        copy.start()

    def base(i, r, j):
        return (xl ^ i) * 24 + ((y + r) % 4) * 6 + (core ^ j) * 3

    pieces = [(r, i, j) for r in range(4) for i in range(2) for j in range(2)]
    planes[25] = jnp.zeros((NY, LANES), f32)
    planes[EVEN] = jnp.zeros((NY, LANES), f32)
    for copy in target_copies:
        copy.wait()

    def members(k):
        if k < 11:
            a = 2 * k + 1
            return (a, a + 1, EVEN + a, EVEN + a + 1)
        return (0, 24, 23, EVEN + 23)

    def products(s):
        for r, i, j in pieces:
            start = base(i, 4 - r, j)
            values = sources[s, 2 * i + j, r]
            source[pl.ds(start, 3)] = values
            product[pl.ds(start, 3)] = values * targets[r, i, j]

    def visit(s):
        for k in range(12):
            if k < 11:
                a = 2 * k + 1
                fa, ga, fb, gb = (product[x] for x in (a, NX - a, a + 1, NX - a - 1))
                rows = [fa + ga, fb + gb, fa - ga, fb - gb]
            else:
                fa, ga = product[23], product[25]
                rows = [product[0], product[24], fa + ga, fa - ga]
            rows = widen(jnp.concatenate(rows, axis=0))
            rows = from_right(rows, table)
            rows = from_left(table, 1, rows).reshape(4, NY, LANES)
            for m, plane in enumerate(members(k)):
                planes[plane] = rows[m]

        for t in range(6):
            band = pl.ds(8 * t, 8)
            screen = widen(filt[0:EVEN, band, :])
            for there, back, lo, size in ((2, 4, 0, EVEN), (3, 5, EVEN, ODD)):
                rows = planes[lo : lo + size, band, :].reshape(size * 8, LANES)
                rows = from_left(table, there, rows)
                rows = rows * screen[:size].reshape(size * 8, LANES)
                rows = from_left(table, back, rows)
                planes[lo : lo + size, band, :] = rows.reshape(size, 8, LANES)

        def add(x, value):
            value = value[:, :NZ] * source[x]
            total[x] = total[x] + value if last else value

        for k in range(12):
            rows = jnp.concatenate([planes[plane] for plane in members(k)], axis=0)
            rows = from_left(table, 1, rows)
            rows = from_right(rows, table).reshape(4, NY, LANES)
            if k < 11:
                a = 2 * k + 1
                for m in range(2):
                    add(a + m, rows[m] + rows[m + 2])
                    add(NX - a - m, rows[m] - rows[m + 2])
            else:
                add(0, rows[0])
                add(24, rows[1])
                add(23, rows[2] + rows[3])
                add(25, rows[2] - rows[3])

    if count == 1:
        for copy in source_copies:
            copy.wait()
        products(0)
        table_copy.wait()
        filt_copy.wait()
        visit(0)
    else:

        @pl.loop(0, count)
        def _(s):
            for q in range(4):
                pltpu.make_async_copy(sources.at[s, q], sources.at[s, q], sems.at[s]).wait()

            @pl.when(s == 0)
            def _():
                table_copy.wait()
                filt_copy.wait()
                for copy in carry_copies:
                    copy.wait()

            products(s)
            visit(s)

    if last:
        homes = {
            (0, 0): keep.at[0], (0, 1): keep.at[1],
            (1, 0): up_second, (1, 1): up_first.at[1],
            (2, 0): up_first.at[0], (2, 1): down_first.at[0],
            (3, 0): down_first.at[1], (3, 1): down_second,
        }
        copies = [
            pltpu.make_async_copy(total.at[pl.ds(base(i, r, j), 3)], homes[r, i].at[j], sems.at[5])
            for r, i, j in pieces
        ]
    else:
        copies = [pltpu.make_async_copy(total, out, sems.at[5])]
    for copy in copies:
        copy.start()
    for copy in copies:
        copy.wait()


def pair_terms(place, target_parts, fields, kernel, table, carried):
    count, last = len(fields), carried is not None
    operands = [place, table, kernel, *target_parts, *[part for field in fields for part in field]]
    whole = jax.ShapeDtypeStruct((2, 2, 3, NY, NZ), f32)
    piece = jax.ShapeDtypeStruct((2, 3, NY, NZ), f32)
    hbm = pl.BlockSpec(memory_space=pl.ANY)
    if last:
        operands.append(carried)
        out_shape, out_specs = [whole, whole, piece, piece, whole], [hbm] * 5
    else:
        out_shape, out_specs = jax.ShapeDtypeStruct((NX, NY, NZ), f32), hbm
    return pl.pallas_call(
        functools.partial(pair_kernel, count, last),
        out_shape=out_shape,
        in_specs=[pl.BlockSpec(memory_space=pltpu.SMEM)] + [hbm] * (len(operands) - 1),
        out_specs=out_specs,
        scratch_shapes=[
            pltpu.VMEM((4, 2, 2, 3, NY, NZ), f32),
            pltpu.VMEM((count, 4, 4, 3, NY, NZ), f32),
            pltpu.VMEM((NX, NY, NZ), f32),
            pltpu.VMEM((NX, NY, NZ), f32),
            pltpu.VMEM((EVEN + ODD, NY, LANES), f32),
            pltpu.VMEM((NX, NY, NZ), f32),
            pltpu.VMEM((FIRST[-1], WIDTH), bf16),
            pltpu.VMEM((EVEN, NY, NZ), f32),
            pltpu.SemaphoreType.DMA((6,)),
        ],
        compiler_params=pltpu.CompilerParams(vmem_limit_bytes=60 * 2**20),
        cost_estimate=pl.CostEstimate(flops=1000, bytes_accessed=1000, transcendentals=0),
        name="pair_terms",
    )(*operands)


def early_kernel(place, orbitals, theirs, own, own_other, near_other, far, lower, upper, stacked, both):
    xh = place[3]
    for n, part in enumerate((own, own_other, near_other, far)):
        stacked[n] = part[...]
    both[pl.ds(4 * xh, 4)] = orbitals[:, :, pl.ds(pl.multiple_of(24 * xh, 8), 24), :]
    both[pl.ds(4 * (1 - xh), 4)] = theirs[...]


def gather_early(place, orbitals, theirs, own, own_other, near_other, far, lower, upper):
    vmem = pl.BlockSpec(memory_space=pltpu.VMEM)
    hbm = pl.BlockSpec(memory_space=pl.ANY)
    return pl.pallas_call(
        early_kernel,
        out_shape=[
            jax.ShapeDtypeStruct((4,) + own.shape, f32),
            jax.ShapeDtypeStruct((8, 3, NY // 2, NZ), f32),
        ],
        in_specs=[pl.BlockSpec(memory_space=pltpu.SMEM)] + [vmem] * 6 + [hbm] * 2,
        out_specs=[vmem] * 2,
        compiler_params=pltpu.CompilerParams(vmem_limit_bytes=12 * 2**20),
        cost_estimate=pl.CostEstimate(flops=1000, bytes_accessed=1000, transcendentals=0),
        name="gather_early",
    )(place, orbitals, theirs, own, own_other, near_other, far, lower, upper)


def late_kernel(near, far_other, total, stacked):
    stacked[0] = near[...]
    stacked[1] = far_other[...]


def gather_late(near, far_other, total):
    vmem = pl.BlockSpec(memory_space=pltpu.VMEM)
    return pl.pallas_call(
        late_kernel,
        out_shape=jax.ShapeDtypeStruct((2,) + near.shape, f32),
        in_specs=[vmem] * 2 + [pl.BlockSpec(memory_space=pl.ANY)],
        out_specs=vmem,
        compiler_params=pltpu.CompilerParams(vmem_limit_bytes=8 * 2**20),
        cost_estimate=pl.CostEstimate(flops=1000, bytes_accessed=1000, transcendentals=0),
        name="gather_late",
    )(near, far_other, total)


def margin_kernel(place, terms, theirs, orbitals, out, sums):
    here = 2 * place[0] + place[2]
    xh = place[3]
    step = pl.program_id(0)

    @pl.loop(0, 8)
    def _(p):
        totals = [[None] * 8 for _ in range(2)]
        for x in range(3):
            for t in range(3):
                rows = pl.ds(8 * t, 8)
                mine = pl.ds(pl.multiple_of(xh * 24 + 8 * t, 8), 8)
                values = [orbitals[2 * p + m, x, rows, :] for m in range(2)]
                for k in range(8):
                    term = terms[k, x, mine, :] if k < 4 else theirs[(k - 4) ^ here, x, rows, :]
                    for m in range(2):
                        value = term * values[m]
                        totals[m][k] = value if totals[m][k] is None else totals[m][k] + value
        for m in range(2):
            for k in range(8):
                sums[k // 4, 2 * p + m, k % 4] = totals[m][k]

    rows = sums[...].reshape(1024, NZ) * (1.0 / GRID)
    high, low = split(rows)
    ones = jnp.ones((NZ, 128), bf16)
    rows = jnp.dot(high, ones, preferred_element_type=f32)
    rows += jnp.dot(low, ones, preferred_element_type=f32)
    rows = jnp.sum(rows.reshape(128, 8, 128), axis=1)
    place_of = lax.broadcasted_iota(jnp.int32, (128, 128), 0)
    lane_of = lax.broadcasted_iota(jnp.int32, (128, 128), 1)
    line = jnp.sum(jnp.where(place_of == lane_of, rows, 0.0), axis=0, keepdims=True)
    for g in range(2):
        row = jnp.broadcast_to(line[:, 64 * g : 64 * g + 64], (16, 64))
        out[pl.ds((xh ^ g) * 16, 16), pl.ds(step, 1), :] = row.reshape(16, 1, 64)


def margin_shares(place, terms, theirs, orbitals):
    vmem = pl.BlockSpec(memory_space=pltpu.VMEM)
    return pl.pallas_call(
        margin_kernel,
        grid=(4,),
        out_shape=jax.ShapeDtypeStruct((32, 4, 64), f32),
        in_specs=[
            pl.BlockSpec(memory_space=pltpu.SMEM),
            vmem,
            vmem,
            pl.BlockSpec((16, 3, NY // 2, NZ), lambda z: (z, 0, 0, 0)),
        ],
        out_specs=pl.BlockSpec((32, 4, 64), lambda z: (0, 0, 0)),
        scratch_shapes=[pltpu.VMEM((2, 16, 4, 8, NZ), f32)],
        compiler_params=pltpu.CompilerParams(vmem_limit_bytes=60 * 2**20),
        cost_estimate=pl.CostEstimate(flops=1000, bytes_accessed=1000, transcendentals=0),
        name="margin_shares",
    )(place, terms, theirs, orbitals)


def moved(array, axes, step):
    size = lax.axis_size(axes)
    return lax.ppermute(array, axes, [(i, (i + step) % size) for i in range(size)])


def pick(array, index):
    return lax.dynamic_index_in_dim(array, index, 0, keepdims=False)


def shifted(array, axes, destination):
    sizes = [lax.axis_size(name) for name in axes]
    pairs = []
    for index in np.ndindex(*sizes):
        goal = destination(*index)
        pairs.append((int(np.ravel_multi_index(index, sizes)), int(np.ravel_multi_index(goal, sizes))))
    return lax.ppermute(array, axes, pairs)


def after(array, other):
    return array + other[(0,) * other.ndim] * 0.0


def local(orbitals, kernel):
    xh, xl, y, core = [lax.axis_index(name) for name in ("xh", "xl", "y", "core")]
    place = jnp.stack([xl, y, core, xh]).astype(jnp.int32)
    table = jnp.asarray(make_table())

    def half(array, h):
        return lax.dynamic_slice_in_dim(array, h * (NY // 2), NY // 2, 2)

    with jax.named_scope("target_slabs"):
        def band(i, j):
            return pick(orbitals, 2 * (xl ^ i) + (core ^ j))

        came = moved(jnp.stack([band(0, 1), band(1, 1)]), "core", 1)
        across = moved(jnp.stack([band(1, 0), came[1]]), "xl", 1)
        part = jnp.stack([jnp.stack([band(0, 0), came[0]]), across])
        lower = moved(part, "y", 1)
        upper = moved(part, "y", -1)
        target_parts = [part, lower, moved(lower[0], "y", 1), moved(upper[1], "y", -1), upper]

    with jax.named_scope("source_slabs"):
        pieces = [pick(orbitals, y)]
        for r in range(1, 4):
            pieces.append(moved(pick(orbitals, (y + r) % 4), "y", r))
        own = after(jnp.stack(pieces), across)

    with jax.named_scope("source_fields"):
        own_other = moved(own, "xl", 1)
        far = moved(own, "z", 1)
        depth = lax.axis_size("z")
        near_other = shifted(own, ("z", "xh", "xl"), lambda k, h, l: ((k + h) % depth, 1 - h, 1 - l))
        near = moved(near_other, "xl", 1)
        far_other = moved(own_other, "z", 1)
        theirs = moved(half(orbitals, 1 - xh), "xh", 1)
        early, both = gather_early(place, orbitals, theirs, own, own_other, near_other, far, lower, upper)
        early = moved(early, "core", 1)

    with jax.named_scope("all_orbitals"):
        everything = lax.all_gather(both, "z", axis=0, tiled=True)

    own_field = [own, early[0], own_other, early[1]]
    total = pair_terms(place, target_parts, [own_field], kernel, table, None)
    late = moved(gather_late(near, far_other, total), "core", 1)
    rest = [[near, late[0], near_other, early[2]], [far, early[3], far_other, late[1]]]
    up, down, up_second, down_second, keep = pair_terms(place, target_parts, rest, kernel, table, total)

    with jax.named_scope("sum_partials"):
        low = moved(up, "y", 1)
        high = moved(down, "y", -1)
        zero = keep[0] + high[1] + moved(up_second + low[0], "y", 1)
        one = keep[1] + low[1] + moved(down_second + high[0], "y", -1)

    with jax.named_scope("to_slabs"):
        came = moved(jnp.stack([zero[1], one[1]]), "core", 1)
        kept = jnp.stack([zero[0], came[0]])
        sent = jnp.stack([one[0], came[1]])
        across = moved(sent, "xl", 1)
        straight = moved(half(kept, 1 - xh), "xh", 1)
        skew = shifted(half(sent, 1 - xh), ("xh", "xl"), lambda h, l: (1 - h, 1 - l))
        theirs = jnp.concatenate([straight, skew])
        relative = jnp.concatenate([kept, across])
        here = 2 * xl + core
        exchange_terms = jnp.stack([pick(relative, b ^ here) for b in range(4)])

    with jax.named_scope("margin"):
        shares = margin_shares(place, exchange_terms, theirs, everything)
        got = lax.all_to_all(shares, ("xh", "xl", "y", "core"), split_axis=0, concat_axis=0, tiled=True)
        margin = jnp.sum(got, axis=0).reshape(64, 4)
    return exchange_terms, margin


def solution(mesh):
    fine = Mesh(mesh.devices.reshape(8, 2, 2, 4, 2), ("z", "xh", "xl", "y", "core"))
    blk = ("z", "xh")
    slab = ("xl", "y", "core")
    return jax.shard_map(
        local,
        mesh=fine,
        in_specs=(P(blk, slab, None, None), P()),
        out_specs=(P(blk, slab, None, None), P(None, blk)),
        check_vma=False,
    )
```

```python
import functools
import math

import jax
import jax.numpy as jnp
import ml_dtypes
import numpy as np
from jax import lax
from jax.experimental import pallas as pl
from jax.experimental.pallas import tpu as pltpu
from jax.sharding import Mesh, PartitionSpec as P

NX = 48
NY = 48
NZ = 240
LANES = 256
EVEN = 26
ODD = 24
GRID = NX * NY * NZ

bf16 = jnp.bfloat16
f32 = jnp.float32
highest = lax.Precision.HIGHEST


def halves(table):
    high = table.astype(ml_dtypes.bfloat16)
    low = (table - high.astype(np.float64)).astype(ml_dtypes.bfloat16)
    return high, low


def cas(length):
    position = np.arange(length)
    angles = (position[:, None] * position[None, :] % length) * (2.0 * math.pi / length)
    return np.cos(angles) + np.sin(angles)


def left_table(table):
    high, low = halves(table)
    return np.concatenate([high, low, high], axis=1)


WIDTH = 3 * LANES
ROWS = (LANES, 192, 8 * EVEN, 8 * ODD, 8 * EVEN, 8 * ODD)
FIRST = tuple(sum(ROWS[:k]) for k in range(len(ROWS) + 1))


def make_table():
    table_z = np.zeros((LANES, LANES))
    table_z[:NZ, :NZ] = cas(NZ)
    high, low = halves(table_z)
    along_z = np.concatenate([high, high, low], axis=1)
    along_y = left_table(np.kron(np.eye(4), cas(NY)))
    place = np.arange(NX // 2 + 1)
    angles = (place[:, None] * place[None, :] % NX) * (2.0 * math.pi / NX)
    even = np.zeros((EVEN, EVEN))
    even[:25, :25] = np.cos(angles)
    odd = np.zeros((ODD, ODD))
    odd[:24, :24] = np.sin(angles)[:24, :24]
    weight = np.full(EVEN, 2.0)
    weight[0] = weight[24] = 1.0
    eye = np.eye(8)
    even_there = left_table(np.kron(even, eye))
    odd_there = left_table(np.kron(odd, eye))
    even_back = left_table(np.kron(even * weight[None, :] * (-1.0 / GRID), eye))
    odd_back = left_table(np.kron(odd * (-2.0 / GRID), eye))
    table = np.zeros((FIRST[-1], WIDTH), ml_dtypes.bfloat16)
    parts = (along_z, along_y, even_there, odd_there, even_back, odd_back)
    for first, part in zip(FIRST, parts):
        table[first : first + part.shape[0], : part.shape[1]] = part
    return table


def split(value):
    high = value.astype(bf16)
    low = (value - high.astype(f32)).astype(bf16)
    return high, low


def from_right(rows, table):
    high, low = split(rows)
    result = jnp.dot(high, table[0:LANES, 0:LANES], preferred_element_type=f32)
    result += jnp.dot(low, table[0:LANES, LANES : 2 * LANES], preferred_element_type=f32)
    return result + jnp.dot(high, table[0:LANES, 2 * LANES :], preferred_element_type=f32)


def from_left(table, k, rows):
    high, low = split(rows)
    stacked = jnp.concatenate([high, high, low], axis=0)
    return jnp.dot(
        table[FIRST[k] : FIRST[k + 1], : stacked.shape[0]], stacked, preferred_element_type=f32
    )


def widen(value):
    return jnp.pad(value, [(0, 0)] * (value.ndim - 1) + [(0, LANES - NZ)])


def pair_kernel(*refs):
    place, table_hbm, filt_hbm = refs[:3]
    target_parts = refs[3:8]
    field_parts = [refs[8 + 4 * s : 12 + 4 * s] for s in range(3)]
    up_first, down_first, up_second, down_second, keep = refs[20:25]
    targets, sources, source, product, planes, total, table, filt, sems = refs[25:]
    xl, y, core = place[0], place[1], place[2]

    table_copy = pltpu.make_async_copy(table_hbm, table, sems.at[3, 0])
    filt_copy = pltpu.make_async_copy(filt_hbm.at[pl.ds(0, EVEN)], filt, sems.at[3, 1])
    homes = (targets.at[0], targets.at[1], targets.at[2, 0], targets.at[2, 1], targets.at[3])
    target_copies = [
        pltpu.make_async_copy(ref, goal, sems.at[4, n]) for n, (ref, goal) in enumerate(zip(target_parts, homes))
    ]
    target_groups = (target_copies[0:1], target_copies[1:2], target_copies[2:4], target_copies[4:5])
    source_copies = [
        [pltpu.make_async_copy(ref.at[r], sources.at[s, r, q], sems.at[s, r]) for q, ref in enumerate(parts)]
        for s, parts in enumerate(field_parts)
        for r in range(4)
    ]
    for r in range(4):
        for copy in target_groups[r]:
            copy.start()
        for copy in source_copies[r]:
            copy.start()
    table_copy.start()
    filt_copy.start()
    for group in source_copies[4:]:
        for copy in group:
            copy.start()

    def base(i, r, j):
        return (xl ^ i) * 24 + ((y + r) % 4) * 6 + (core ^ j) * 3

    pieces = [(r, i, j) for r in range(4) for i in range(2) for j in range(2)]
    planes[25] = jnp.zeros((NY, LANES), f32)
    planes[EVEN] = jnp.zeros((NY, LANES), f32)
    total[...] = jnp.zeros_like(total)

    def members(k):
        if k < 11:
            a = 2 * k + 1
            return (a, a + 1, EVEN + a, EVEN + a + 1)
        return (0, 24, 23, EVEN + 23)

    def products(s):
        for r in range(4):

            @pl.when(s == 0)
            def _():
                for copy in target_groups[r]:
                    copy.wait()

            for q in range(4):
                pltpu.make_async_copy(sources.at[s, r, q], sources.at[s, r, q], sems.at[s, r]).wait()
            for i in range(2):
                for j in range(2):
                    start = base(i, 4 - r, j)
                    values = sources[s, r, 2 * i + j]
                    source[pl.ds(start, 3)] = values
                    product[pl.ds(start, 3)] = values * targets[r, i, j]

    def visit(s):
        for k in range(12):
            if k < 11:
                a = 2 * k + 1
                fa, ga, fb, gb = (product[x] for x in (a, NX - a, a + 1, NX - a - 1))
                rows = [fa + ga, fb + gb, fa - ga, fb - gb]
            else:
                fa, ga = product[23], product[25]
                rows = [product[0], product[24], fa + ga, fa - ga]
            rows = widen(jnp.concatenate(rows, axis=0))
            rows = from_right(rows, table)
            rows = from_left(table, 1, rows).reshape(4, NY, LANES)
            for m, plane in enumerate(members(k)):
                planes[plane] = rows[m]

        for t in range(6):
            band = pl.ds(8 * t, 8)
            screen = widen(filt[0:EVEN, band, :])
            for there, back, lo, size in ((2, 4, 0, EVEN), (3, 5, EVEN, ODD)):
                rows = planes[lo : lo + size, band, :].reshape(size * 8, LANES)
                rows = from_left(table, there, rows)
                rows = rows * screen[:size].reshape(size * 8, LANES)
                rows = from_left(table, back, rows)
                planes[lo : lo + size, band, :] = rows.reshape(size, 8, LANES)

        def add(x, value):
            value = value[:, :NZ] * source[x]
            total[x] += value

        for k in range(12):
            rows = jnp.concatenate([planes[plane] for plane in members(k)], axis=0)
            rows = from_left(table, 1, rows)
            rows = from_right(rows, table).reshape(4, NY, LANES)
            if k < 11:
                a = 2 * k + 1
                for m in range(2):
                    add(a + m, rows[m] + rows[m + 2])
                    add(NX - a - m, rows[m] - rows[m + 2])
            else:
                add(0, rows[0])
                add(24, rows[1])
                add(23, rows[2] + rows[3])
                add(25, rows[2] - rows[3])

    @pl.loop(0, 3)
    def _(s):
        products(s)

        @pl.when(s == 0)
        def _():
            table_copy.wait()
            filt_copy.wait()

        visit(s)

    homes = {
        (0, 0): keep.at[0], (0, 1): keep.at[1],
        (1, 0): up_second, (1, 1): up_first.at[1],
        (2, 0): up_first.at[0], (2, 1): down_first.at[0],
        (3, 0): down_first.at[1], (3, 1): down_second,
    }
    copies = [
        pltpu.make_async_copy(total.at[pl.ds(base(i, r, j), 3)], homes[r, i].at[j], sems.at[3, 2])
        for r, i, j in pieces
    ]
    for copy in copies:
        copy.start()
    for copy in copies:
        copy.wait()


def pair_terms(place, target_parts, fields, kernel, table):
    operands = [place, table, kernel, *target_parts, *[part for field in fields for part in field]]
    whole = jax.ShapeDtypeStruct((2, 2, 3, NY, NZ), f32)
    piece = jax.ShapeDtypeStruct((2, 3, NY, NZ), f32)
    hbm = pl.BlockSpec(memory_space=pl.ANY)
    return pl.pallas_call(
        pair_kernel,
        out_shape=[whole, whole, piece, piece, whole],
        in_specs=[pl.BlockSpec(memory_space=pltpu.SMEM)] + [hbm] * (len(operands) - 1),
        out_specs=[hbm] * 5,
        scratch_shapes=[
            pltpu.VMEM((4, 2, 2, 3, NY, NZ), f32),
            pltpu.VMEM((3, 4, 4, 3, NY, NZ), f32),
            pltpu.VMEM((NX, NY, NZ), f32),
            pltpu.VMEM((NX, NY, NZ), f32),
            pltpu.VMEM((EVEN + ODD, NY, LANES), f32),
            pltpu.VMEM((NX, NY, NZ), f32),
            pltpu.VMEM((FIRST[-1], WIDTH), bf16),
            pltpu.VMEM((EVEN, NY, NZ), f32),
            pltpu.SemaphoreType.DMA((5, 5)),
        ],
        compiler_params=pltpu.CompilerParams(vmem_limit_bytes=60 * 2**20),
        cost_estimate=pl.CostEstimate(flops=1000, bytes_accessed=1000, transcendentals=0),
        name="pair_terms",
    )(*operands)


def halves_kernel(place, orbitals, theirs, *refs):
    both, sems = refs[-2:]
    xh = place[3]
    mine = orbitals.at[:, :, pl.ds(pl.multiple_of(24 * xh, 8), 24), :]
    copies = [
        pltpu.make_async_copy(mine, both.at[pl.ds(4 * xh, 4)], sems.at[0]),
        pltpu.make_async_copy(theirs, both.at[pl.ds(4 * (1 - xh), 4)], sems.at[1]),
    ]
    for copy in copies:
        copy.start()
    for copy in copies:
        copy.wait()


def both_halves(place, orbitals, theirs, *events):
    vmem = pl.BlockSpec(memory_space=pltpu.VMEM)
    hbm = pl.BlockSpec(memory_space=pl.ANY)
    return pl.pallas_call(
        halves_kernel,
        out_shape=jax.ShapeDtypeStruct((8, 3, NY // 2, NZ), f32),
        in_specs=[pl.BlockSpec(memory_space=pltpu.SMEM), vmem, vmem] + [hbm] * len(events),
        out_specs=hbm,
        scratch_shapes=[pltpu.SemaphoreType.DMA((2,))],
        compiler_params=pltpu.CompilerParams(vmem_limit_bytes=60 * 2**20),
        cost_estimate=pl.CostEstimate(flops=1000, bytes_accessed=1000, transcendentals=0),
        name="both_halves",
    )(place, orbitals, theirs, *events)


def margin_kernel(place, kept, across, straight, skew, orbitals, shares, exchange, sums, lines, sems):
    here = 2 * place[0] + place[2]
    xh = place[3]
    step = pl.program_id(0)
    copies = [
        pltpu.make_async_copy(pair.at[b], exchange.at[(2 * a + b) ^ here], sems.at[2 * a + b])
        for a, pair in enumerate((kept, across))
        for b in range(2)
    ]

    @pl.when(step == 0)
    def _():
        for copy in copies:
            copy.start()

    @pl.loop(0, 16)
    def _(p):
        totals = [[None] * 8 for _ in range(2)]
        for x in range(3):
            for t in range(3):
                rows = pl.ds(8 * t, 8)
                mine = pl.ds(pl.multiple_of(xh * 24 + 8 * t, 8), 8)
                values = [orbitals[2 * p + m, x, rows, :] for m in range(2)]
                terms = [kept[0, x, mine, :], kept[1, x, mine, :], across[0, x, mine, :], across[1, x, mine, :]]
                terms += [straight[0, x, rows, :], straight[1, x, rows, :], skew[0, x, rows, :], skew[1, x, rows, :]]
                for k in range(8):
                    for m in range(2):
                        value = terms[k] * values[m]
                        totals[m][k] = value if totals[m][k] is None else totals[m][k] + value
        for m in range(2):
            for k in range(8):
                sums[k // 4, 2 * p + m, (k % 4) ^ here] = totals[m][k]

    rows = sums[...].reshape(2048, NZ) * (1.0 / GRID)
    high, low = split(rows)
    ones = jnp.ones((NZ, 128), bf16)
    rows = jnp.dot(high, ones, preferred_element_type=f32)
    rows += jnp.dot(low, ones, preferred_element_type=f32)
    rows = jnp.sum(rows.reshape(256, 8, 128), axis=1)
    place_of = lax.broadcasted_iota(jnp.int32, (128, 128), 0)
    lane_of = lax.broadcasted_iota(jnp.int32, (128, 128), 1)
    for g in range(2):
        line = jnp.where(place_of == lane_of, rows[128 * g : 128 * g + 128], 0.0)
        lines[g, pl.ds(step, 1)] = jnp.sum(line, axis=0, keepdims=True)

    @pl.when(step == 1)
    def _():
        for g in range(2):
            for n in range(2):
                row = jnp.broadcast_to(lines[g, n : n + 1], (16, 128))
                shares[pl.ds((xh ^ g) * 16, 16), 0, 128 * n : 128 * n + 128] = row
        for copy in copies:
            copy.wait()


def margin_shares(place, kept, across, straight, skew, orbitals):
    vmem = pl.BlockSpec(memory_space=pltpu.VMEM)
    return pl.pallas_call(
        margin_kernel,
        grid=(2,),
        out_shape=[
            jax.ShapeDtypeStruct((32, 1, 256), f32),
            jax.ShapeDtypeStruct((4, 3, NY, NZ), f32),
        ],
        in_specs=[pl.BlockSpec(memory_space=pltpu.SMEM)]
        + [vmem] * 4
        + [pl.BlockSpec((32, 3, NY // 2, NZ), lambda z: (z, 0, 0, 0))],
        out_specs=[
            pl.BlockSpec((32, 1, 256), lambda z: (0, 0, 0)),
            pl.BlockSpec(memory_space=pl.ANY),
        ],
        scratch_shapes=[
            pltpu.VMEM((2, 32, 4, 8, NZ), f32),
            pltpu.VMEM((2, 2, 128), f32),
            pltpu.SemaphoreType.DMA((4,)),
        ],
        compiler_params=pltpu.CompilerParams(vmem_limit_bytes=60 * 2**20),
        cost_estimate=pl.CostEstimate(flops=1000, bytes_accessed=1000, transcendentals=0),
        name="margin_shares",
    )(place, kept, across, straight, skew, orbitals)


def moved(array, axes, step):
    size = lax.axis_size(axes)
    return lax.ppermute(array, axes, [(i, (i + step) % size) for i in range(size)])


def pick(array, index):
    return lax.dynamic_index_in_dim(array, index, 0, keepdims=False)


def shifted(array, axes, destination):
    sizes = [lax.axis_size(name) for name in axes]
    pairs = []
    for index in np.ndindex(*sizes):
        goal = destination(*index)
        pairs.append((int(np.ravel_multi_index(index, sizes)), int(np.ravel_multi_index(goal, sizes))))
    return lax.ppermute(array, axes, pairs)


def after(array, other):
    return array + other[(0,) * other.ndim] * 0.0


def local(orbitals, kernel):
    xh, xl, y, core = [lax.axis_index(name) for name in ("xh", "xl", "y", "core")]
    place = jnp.stack([xl, y, core, xh]).astype(jnp.int32)
    table = jnp.asarray(make_table())

    def half(array, h):
        return lax.dynamic_slice_in_dim(array, h * (NY // 2), NY // 2, 2)

    with jax.named_scope("source_slabs"):
        pieces = [pick(orbitals, y)]
        for r in range(1, 4):
            pieces.append(moved(pick(orbitals, (y + r) % 4), "y", r))

    with jax.named_scope("all_orbitals"):
        theirs = moved(half(orbitals, 1 - xh), "xh", 1)

    with jax.named_scope("target_slabs"):
        def band(i, j):
            return pick(orbitals, 2 * (xl ^ i) + (core ^ j))

        came = moved(jnp.stack([band(0, 1), band(1, 1)]), "core", 1)
        across = moved(jnp.stack([band(1, 0), came[1]]), "xl", 1)
        part = jnp.stack([jnp.stack([band(0, 0), came[0]]), across])
        part = after(after(part, pieces[2]), theirs)
        lower = moved(part, "y", 1)
        upper = moved(part, "y", -1)
        target_parts = [part, lower, moved(lower[0], "y", 1), moved(upper[1], "y", -1), upper]

    own = after(jnp.stack(pieces), across)

    with jax.named_scope("source_fields"):
        own_other = moved(own, "xl", 1)
        far = moved(own, "z", 1)
        depth = lax.axis_size("z")
        near_other = shifted(own, ("z", "xh", "xl"), lambda k, h, l: ((k + h) % depth, 1 - h, 1 - l))
        near = moved(near_other, "xl", 1)
        far_other = moved(own_other, "z", 1)
        fields = []
        for slabs, other in ((own, own_other), (near, near_other), (far, far_other)):
            fields.append([slabs, moved(slabs, "core", 1), other, moved(other, "core", 1)])

    with jax.named_scope("all_orbitals"):
        events = [*target_parts, *[part for field in fields for part in field]]
        both = both_halves(place, orbitals, theirs, *events)
        everything = lax.all_gather(both, "z", axis=0, tiled=True)

    up, down, up_second, down_second, keep = pair_terms(place, target_parts, fields, kernel, table)

    with jax.named_scope("sum_partials"):
        low = moved(up, "y", 1)
        high = moved(down, "y", -1)
        zero = keep[0] + high[1] + moved(up_second + low[0], "y", 1)
        one = keep[1] + low[1] + moved(down_second + high[0], "y", -1)

    with jax.named_scope("to_slabs"):
        came = moved(jnp.stack([zero[1], one[1]]), "core", 1)
        kept = jnp.stack([zero[0], came[0]])
        sent = jnp.stack([one[0], came[1]])
        across = moved(sent, "xl", 1)
        straight = moved(half(kept, 1 - xh), "xh", 1)
        skew = shifted(half(sent, 1 - xh), ("xh", "xl"), lambda h, l: (1 - h, 1 - l))

    with jax.named_scope("margin"):
        shares, exchange_terms = margin_shares(place, kept, across, straight, skew, everything)
        got = lax.all_to_all(shares, ("xh", "xl", "y", "core"), split_axis=0, concat_axis=0, tiled=True)
        margin = jnp.sum(got, axis=0).reshape(64, 4)
    return exchange_terms, margin


def solution(mesh):
    fine = Mesh(mesh.devices.reshape(8, 2, 2, 4, 2), ("z", "xh", "xl", "y", "core"))
    blk = ("z", "xh")
    slab = ("xl", "y", "core")
    return jax.shard_map(
        local,
        mesh=fine,
        in_specs=(P(blk, slab, None, None), P()),
        out_specs=(P(blk, slab, None, None), P(None, blk)),
        check_vma=False,
    )
```

```python
import functools
import math

import jax
import jax.numpy as jnp
import ml_dtypes
import numpy as np
from jax import lax
from jax.experimental import pallas as pl
from jax.experimental.pallas import tpu as pltpu
from jax.sharding import Mesh, PartitionSpec as P

NX = 48
NY = 48
NZ = 240
LANES = 256
EVEN = 26
ODD = 24
GRID = NX * NY * NZ

bf16 = jnp.bfloat16
f32 = jnp.float32
highest = lax.Precision.HIGHEST


def halves(table):
    high = table.astype(ml_dtypes.bfloat16)
    low = (table - high.astype(np.float64)).astype(ml_dtypes.bfloat16)
    return high, low


def cas(length):
    position = np.arange(length)
    angles = (position[:, None] * position[None, :] % length) * (2.0 * math.pi / length)
    return np.cos(angles) + np.sin(angles)


def left_table(table):
    high, low = halves(table)
    return np.concatenate([high, low, high], axis=1)


WIDTH = 3 * LANES
ROWS = (LANES, 192, 8 * EVEN, 8 * ODD, 8 * EVEN, 8 * ODD)
FIRST = tuple(sum(ROWS[:k]) for k in range(len(ROWS) + 1))


def make_table():
    table_z = np.zeros((LANES, LANES))
    table_z[:NZ, :NZ] = cas(NZ)
    high, low = halves(table_z)
    along_z = np.concatenate([high, high, low], axis=1)
    along_y = left_table(np.kron(np.eye(4), cas(NY)))
    place = np.arange(NX // 2 + 1)
    angles = (place[:, None] * place[None, :] % NX) * (2.0 * math.pi / NX)
    even = np.zeros((EVEN, EVEN))
    even[:25, :25] = np.cos(angles)
    odd = np.zeros((ODD, ODD))
    odd[:24, :24] = np.sin(angles)[:24, :24]
    weight = np.full(EVEN, 2.0)
    weight[0] = weight[24] = 1.0
    eye = np.eye(8)
    even_there = left_table(np.kron(even, eye))
    odd_there = left_table(np.kron(odd, eye))
    even_back = left_table(np.kron(even * weight[None, :] * (-1.0 / GRID), eye))
    odd_back = left_table(np.kron(odd * (-2.0 / GRID), eye))
    table = np.zeros((FIRST[-1], WIDTH), ml_dtypes.bfloat16)
    parts = (along_z, along_y, even_there, odd_there, even_back, odd_back)
    for first, part in zip(FIRST, parts):
        table[first : first + part.shape[0], : part.shape[1]] = part
    return table


def split(value):
    high = value.astype(bf16)
    low = (value - high.astype(f32)).astype(bf16)
    return high, low


def from_right(rows, table):
    high, low = split(rows)
    result = jnp.dot(high, table[0:LANES, 0:LANES], preferred_element_type=f32)
    result += jnp.dot(low, table[0:LANES, LANES : 2 * LANES], preferred_element_type=f32)
    return result + jnp.dot(high, table[0:LANES, 2 * LANES :], preferred_element_type=f32)


def from_left(table, k, rows):
    high, low = split(rows)
    stacked = jnp.concatenate([high, high, low], axis=0)
    return jnp.dot(
        table[FIRST[k] : FIRST[k + 1], : stacked.shape[0]], stacked, preferred_element_type=f32
    )


def widen(value):
    return jnp.pad(value, [(0, 0)] * (value.ndim - 1) + [(0, LANES - NZ)])


def pair_kernel(*refs):
    place, table_hbm, filt_hbm = refs[:3]
    target_parts = refs[3:8]
    field_parts = [refs[8 + 4 * s : 12 + 4 * s] for s in range(3)]
    up_first, down_first, up_second, down_second, keep = refs[20:25]
    targets, sources, source, product, planes, total, table, filt, sems = refs[25:]
    xl, y, core = place[0], place[1], place[2]

    table_copy = pltpu.make_async_copy(table_hbm, table, sems.at[3, 0])
    filt_copy = pltpu.make_async_copy(filt_hbm.at[pl.ds(0, EVEN)], filt, sems.at[3, 1])
    homes = (targets.at[0], targets.at[1], targets.at[2, 0], targets.at[2, 1], targets.at[3])
    target_copies = [
        pltpu.make_async_copy(ref, goal, sems.at[4, n]) for n, (ref, goal) in enumerate(zip(target_parts, homes))
    ]
    target_groups = (target_copies[0:1], target_copies[1:2], target_copies[2:4], target_copies[4:5])
    source_copies = [
        [pltpu.make_async_copy(ref.at[r], sources.at[s, r, q], sems.at[s, r]) for q, ref in enumerate(parts)]
        for s, parts in enumerate(field_parts)
        for r in range(4)
    ]
    for r in range(4):
        for copy in target_groups[r]:
            copy.start()
        for copy in source_copies[r]:
            copy.start()
    table_copy.start()
    filt_copy.start()
    for group in source_copies[4:]:
        for copy in group:
            copy.start()

    def base(i, r, j):
        return (xl ^ i) * 24 + ((y + r) % 4) * 6 + (core ^ j) * 3

    pieces = [(r, i, j) for r in range(4) for i in range(2) for j in range(2)]
    planes[25] = jnp.zeros((NY, LANES), f32)
    planes[EVEN] = jnp.zeros((NY, LANES), f32)
    total[...] = jnp.zeros_like(total)

    def members(k):
        if k < 11:
            a = 2 * k + 1
            return (a, a + 1, EVEN + a, EVEN + a + 1)
        return (0, 24, 23, EVEN + 23)

    def products(s):
        for r in range(4):

            @pl.when(s == 0)
            def _():
                for copy in target_groups[r]:
                    copy.wait()

            for q in range(4):
                pltpu.make_async_copy(sources.at[s, r, q], sources.at[s, r, q], sems.at[s, r]).wait()
            for i in range(2):
                for j in range(2):
                    start = base(i, 4 - r, j)
                    values = sources[s, r, 2 * i + j]
                    source[pl.ds(start, 3)] = values
                    product[pl.ds(start, 3)] = values * targets[r, i, j]

    def visit(s):
        for k in range(12):
            if k < 11:
                a = 2 * k + 1
                fa, ga, fb, gb = (product[x] for x in (a, NX - a, a + 1, NX - a - 1))
                rows = [fa + ga, fb + gb, fa - ga, fb - gb]
            else:
                fa, ga = product[23], product[25]
                rows = [product[0], product[24], fa + ga, fa - ga]
            rows = widen(jnp.concatenate(rows, axis=0))
            rows = from_right(rows, table)
            rows = from_left(table, 1, rows).reshape(4, NY, LANES)
            for m, plane in enumerate(members(k)):
                planes[plane] = rows[m]

        for t in range(6):
            band = pl.ds(8 * t, 8)
            screen = widen(filt[0:EVEN, band, :])
            for there, back, lo, size in ((2, 4, 0, EVEN), (3, 5, EVEN, ODD)):
                rows = planes[lo : lo + size, band, :].reshape(size * 8, LANES)
                rows = from_left(table, there, rows)
                rows = rows * screen[:size].reshape(size * 8, LANES)
                rows = from_left(table, back, rows)
                planes[lo : lo + size, band, :] = rows.reshape(size, 8, LANES)

        def add(x, value):
            value = value[:, :NZ] * source[x]
            total[x] += value

        for k in range(12):
            rows = jnp.concatenate([planes[plane] for plane in members(k)], axis=0)
            rows = from_left(table, 1, rows)
            rows = from_right(rows, table).reshape(4, NY, LANES)
            if k < 11:
                a = 2 * k + 1
                for m in range(2):
                    add(a + m, rows[m] + rows[m + 2])
                    add(NX - a - m, rows[m] - rows[m + 2])
            else:
                add(0, rows[0])
                add(24, rows[1])
                add(23, rows[2] + rows[3])
                add(25, rows[2] - rows[3])

    @pl.loop(0, 3)
    def _(s):
        products(s)

        @pl.when(s == 0)
        def _():
            table_copy.wait()
            filt_copy.wait()

        visit(s)

    homes = {
        (0, 0): keep.at[0], (0, 1): keep.at[1],
        (1, 0): up_second, (1, 1): up_first.at[1],
        (2, 0): up_first.at[0], (2, 1): down_first.at[0],
        (3, 0): down_first.at[1], (3, 1): down_second,
    }
    copies = [
        pltpu.make_async_copy(total.at[pl.ds(base(i, r, j), 3)], homes[r, i].at[j], sems.at[3, 2])
        for r, i, j in pieces
    ]
    for copy in copies:
        copy.start()
    for copy in copies:
        copy.wait()


def pair_terms(place, target_parts, fields, kernel, table):
    operands = [place, table, kernel, *target_parts, *[part for field in fields for part in field]]
    whole = jax.ShapeDtypeStruct((2, 2, 3, NY, NZ), f32)
    piece = jax.ShapeDtypeStruct((2, 3, NY, NZ), f32)
    hbm = pl.BlockSpec(memory_space=pl.ANY)
    return pl.pallas_call(
        pair_kernel,
        out_shape=[whole, whole, piece, piece, whole],
        in_specs=[pl.BlockSpec(memory_space=pltpu.SMEM)] + [hbm] * (len(operands) - 1),
        out_specs=[hbm] * 5,
        scratch_shapes=[
            pltpu.VMEM((4, 2, 2, 3, NY, NZ), f32),
            pltpu.VMEM((3, 4, 4, 3, NY, NZ), f32),
            pltpu.VMEM((NX, NY, NZ), f32),
            pltpu.VMEM((NX, NY, NZ), f32),
            pltpu.VMEM((EVEN + ODD, NY, LANES), f32),
            pltpu.VMEM((NX, NY, NZ), f32),
            pltpu.VMEM((FIRST[-1], WIDTH), bf16),
            pltpu.VMEM((EVEN, NY, NZ), f32),
            pltpu.SemaphoreType.DMA((5, 5)),
        ],
        compiler_params=pltpu.CompilerParams(vmem_limit_bytes=60 * 2**20),
        cost_estimate=pl.CostEstimate(flops=1000, bytes_accessed=1000, transcendentals=0),
        name="pair_terms",
    )(*operands)


def halves_kernel(place, orbitals, theirs, *refs):
    both, sems = refs[-2:]
    xh = place[3]
    mine = orbitals.at[:, :, pl.ds(pl.multiple_of(24 * xh, 8), 24), :]
    copies = [
        pltpu.make_async_copy(mine, both.at[pl.ds(4 * xh, 4)], sems.at[0]),
        pltpu.make_async_copy(theirs, both.at[pl.ds(4 * (1 - xh), 4)], sems.at[1]),
    ]
    for copy in copies:
        copy.start()
    for copy in copies:
        copy.wait()


def both_halves(place, orbitals, theirs, *events):
    vmem = pl.BlockSpec(memory_space=pltpu.VMEM)
    hbm = pl.BlockSpec(memory_space=pl.ANY)
    return pl.pallas_call(
        halves_kernel,
        out_shape=jax.ShapeDtypeStruct((8, 3, NY // 2, NZ), f32),
        in_specs=[pl.BlockSpec(memory_space=pltpu.SMEM), vmem, vmem] + [hbm] * len(events),
        out_specs=hbm,
        scratch_shapes=[pltpu.SemaphoreType.DMA((2,))],
        compiler_params=pltpu.CompilerParams(vmem_limit_bytes=60 * 2**20),
        cost_estimate=pl.CostEstimate(flops=1000, bytes_accessed=1000, transcendentals=0),
        name="both_halves",
    )(place, orbitals, theirs, *events)


def held_kernel(*refs):
    del refs


def held_until(array, *events):
    hbm = pl.BlockSpec(memory_space=pl.ANY)
    return pl.pallas_call(
        held_kernel,
        out_shape=jax.ShapeDtypeStruct(array.shape, array.dtype),
        in_specs=[hbm] * (1 + len(events)),
        out_specs=hbm,
        input_output_aliases={0: 0},
        compiler_params=pltpu.CompilerParams(vmem_limit_bytes=60 * 2**20),
        cost_estimate=pl.CostEstimate(flops=1000, bytes_accessed=1000, transcendentals=0),
        name="held_until",
    )(array, *events)


def margin_kernel(place, kept, across, straight, skew, orbitals, shares, exchange, sums, lines, sems):
    here = 2 * place[0] + place[2]
    xh = place[3]
    step = pl.program_id(0)
    copies = [
        pltpu.make_async_copy(pair.at[b], exchange.at[(2 * a + b) ^ here], sems.at[2 * a + b])
        for a, pair in enumerate((kept, across))
        for b in range(2)
    ]

    @pl.when(step == 0)
    def _():
        for copy in copies:
            copy.start()

    @pl.loop(0, 16)
    def _(p):
        totals = [[None] * 8 for _ in range(2)]
        for x in range(3):
            for t in range(3):
                rows = pl.ds(8 * t, 8)
                mine = pl.ds(pl.multiple_of(xh * 24 + 8 * t, 8), 8)
                values = [orbitals[2 * p + m, x, rows, :] for m in range(2)]
                terms = [kept[0, x, mine, :], kept[1, x, mine, :], across[0, x, mine, :], across[1, x, mine, :]]
                terms += [straight[0, x, rows, :], straight[1, x, rows, :], skew[0, x, rows, :], skew[1, x, rows, :]]
                for k in range(8):
                    for m in range(2):
                        value = terms[k] * values[m]
                        totals[m][k] = value if totals[m][k] is None else totals[m][k] + value
        for m in range(2):
            for k in range(8):
                sums[k // 4, 2 * p + m, (k % 4) ^ here] = totals[m][k]

    rows = sums[...].reshape(2048, NZ) * (1.0 / GRID)
    high, low = split(rows)
    ones = jnp.ones((NZ, 128), bf16)
    rows = jnp.dot(high, ones, preferred_element_type=f32)
    rows += jnp.dot(low, ones, preferred_element_type=f32)
    rows = jnp.sum(rows.reshape(256, 8, 128), axis=1)
    place_of = lax.broadcasted_iota(jnp.int32, (128, 128), 0)
    lane_of = lax.broadcasted_iota(jnp.int32, (128, 128), 1)
    for g in range(2):
        line = jnp.where(place_of == lane_of, rows[128 * g : 128 * g + 128], 0.0)
        lines[g, pl.ds(step, 1)] = jnp.sum(line, axis=0, keepdims=True)

    @pl.when(step == 1)
    def _():
        for g in range(2):
            for n in range(2):
                row = jnp.broadcast_to(lines[g, n : n + 1], (16, 128))
                shares[pl.ds((xh ^ g) * 16, 16), 0, 128 * n : 128 * n + 128] = row
        for copy in copies:
            copy.wait()


def margin_shares(place, kept, across, straight, skew, orbitals):
    vmem = pl.BlockSpec(memory_space=pltpu.VMEM)
    return pl.pallas_call(
        margin_kernel,
        grid=(2,),
        out_shape=[
            jax.ShapeDtypeStruct((32, 1, 256), f32),
            jax.ShapeDtypeStruct((4, 3, NY, NZ), f32),
        ],
        in_specs=[pl.BlockSpec(memory_space=pltpu.SMEM)]
        + [vmem] * 4
        + [pl.BlockSpec((32, 3, NY // 2, NZ), lambda z: (z, 0, 0, 0))],
        out_specs=[
            pl.BlockSpec((32, 1, 256), lambda z: (0, 0, 0)),
            pl.BlockSpec(memory_space=pl.ANY),
        ],
        scratch_shapes=[
            pltpu.VMEM((2, 32, 4, 8, NZ), f32),
            pltpu.VMEM((2, 2, 128), f32),
            pltpu.SemaphoreType.DMA((4,)),
        ],
        compiler_params=pltpu.CompilerParams(vmem_limit_bytes=60 * 2**20),
        cost_estimate=pl.CostEstimate(flops=1000, bytes_accessed=1000, transcendentals=0),
        name="margin_shares",
    )(place, kept, across, straight, skew, orbitals)


def moved(array, axes, step):
    size = lax.axis_size(axes)
    return lax.ppermute(array, axes, [(i, (i + step) % size) for i in range(size)])


def pick(array, index):
    return lax.dynamic_index_in_dim(array, index, 0, keepdims=False)


def shifted(array, axes, destination):
    sizes = [lax.axis_size(name) for name in axes]
    pairs = []
    for index in np.ndindex(*sizes):
        goal = destination(*index)
        pairs.append((int(np.ravel_multi_index(index, sizes)), int(np.ravel_multi_index(goal, sizes))))
    return lax.ppermute(array, axes, pairs)


def after(array, other):
    return array + other[(0,) * other.ndim] * 0.0


def local(orbitals, kernel):
    xh, xl, y, core = [lax.axis_index(name) for name in ("xh", "xl", "y", "core")]
    place = jnp.stack([xl, y, core, xh]).astype(jnp.int32)
    table = jnp.asarray(make_table())

    def half(array, h):
        return lax.dynamic_slice_in_dim(array, h * (NY // 2), NY // 2, 2)

    with jax.named_scope("source_slabs"):
        pieces = [pick(orbitals, y)]
        for r in range(1, 4):
            pieces.append(moved(pick(orbitals, (y + r) % 4), "y", r))

    with jax.named_scope("all_orbitals"):
        theirs = moved(half(orbitals, 1 - xh), "xh", 1)
        both = both_halves(place, orbitals, theirs)

    with jax.named_scope("target_slabs"):
        def band(i, j):
            return pick(orbitals, 2 * (xl ^ i) + (core ^ j))

        came = moved(jnp.stack([band(0, 1), band(1, 1)]), "core", 1)
        across = moved(jnp.stack([band(1, 0), came[1]]), "xl", 1)
        part = jnp.stack([jnp.stack([band(0, 0), came[0]]), across])
        part = after(after(part, pieces[2]), both)
        lower = moved(part, "y", 1)
        upper = moved(part, "y", -1)
        target_parts = [part, lower, moved(lower[0], "y", 1), moved(upper[1], "y", -1), upper]

    own = after(jnp.stack(pieces), across)

    with jax.named_scope("source_fields"):
        own_other = moved(own, "xl", 1)
        far = moved(own, "z", 1)
        depth = lax.axis_size("z")
        near_other = shifted(own, ("z", "xh", "xl"), lambda k, h, l: ((k + h) % depth, 1 - h, 1 - l))
        near = moved(near_other, "xl", 1)
        far_other = moved(own_other, "z", 1)
        fields = []
        for slabs, other in ((own, own_other), (near, near_other), (far, far_other)):
            fields.append([slabs, moved(slabs, "core", 1), other, moved(other, "core", 1)])

    with jax.named_scope("all_orbitals"):
        events = [*target_parts, *[part for field in fields for part in field]]
        everything = lax.all_gather(held_until(both, *events), "z", axis=0, tiled=True)

    up, down, up_second, down_second, keep = pair_terms(place, target_parts, fields, kernel, table)

    with jax.named_scope("sum_partials"):
        low = moved(up, "y", 1)
        high = moved(down, "y", -1)
        zero = keep[0] + high[1] + moved(up_second + low[0], "y", 1)
        one = keep[1] + low[1] + moved(down_second + high[0], "y", -1)

    with jax.named_scope("to_slabs"):
        came = moved(jnp.stack([zero[1], one[1]]), "core", 1)
        kept = jnp.stack([zero[0], came[0]])
        sent = jnp.stack([one[0], came[1]])
        across = moved(sent, "xl", 1)
        straight = moved(half(kept, 1 - xh), "xh", 1)
        skew = shifted(half(sent, 1 - xh), ("xh", "xl"), lambda h, l: (1 - h, 1 - l))

    with jax.named_scope("margin"):
        shares, exchange_terms = margin_shares(place, kept, across, straight, skew, everything)
        got = lax.all_to_all(shares, ("xh", "xl", "y", "core"), split_axis=0, concat_axis=0, tiled=True)
        margin = jnp.sum(got, axis=0).reshape(64, 4)
    return exchange_terms, margin


def solution(mesh):
    fine = Mesh(mesh.devices.reshape(8, 2, 2, 4, 2), ("z", "xh", "xl", "y", "core"))
    blk = ("z", "xh")
    slab = ("xl", "y", "core")
    return jax.shard_map(
        local,
        mesh=fine,
        in_specs=(P(blk, slab, None, None), P()),
        out_specs=(P(blk, slab, None, None), P(None, blk)),
        check_vma=False,
    )
```
